32 devices in a mesh: grp: 2 (over y), gz: 4 (over x, core), gx: 4 (over z).
Axes of the slice: x: 2, y: 2, z: 4, core: 2. Of those that a mesh axis runs over, the one named last changes fastest.
Arguments:
- volume: float32 [128, 512, 512], P(('grp', 'gz'), 'gx'), parts along dimension 0, may hold values from -6 to 6
- col_weight: bfloat16 [64, 512, 512], P('gz', 'gx'), may hold values from 0.5 to 2
- column_map: bfloat16 [2, 512, 2048], P(None, 'gx'), may hold values from -0.25 to 0.25
- depth_map: bfloat16 [2, 512, 384], replicated, may hold values from -0.0625 to 0.0625
- measured: float32 [4096, 2, 512], P(('grp', 'gx'), None, 'gz'), parts along dimension 0, may hold values from -6 to 6
- row_weight: float32 [2048, 2, 512], P('gx', None, 'gz'), may hold values from 0.5 to 2
- band_start: int32 [2, 64], P(None, 'gz'), may hold values from 0 to 384, as said below
- band_len: int32 [2, 64], P(None, 'gz'), may hold values from 128 to 384, as said below
Outputs:
- updated_volume: float32 [128, 512, 512], P(('grp', 'gz'), 'gx'), parts along dimension 0
The draws below stay inside these ranges and needn't reach their ends.
There are 2 independent parts, one for each index of `grp`. The reference program is written for one: setup_inputs(seed, part) draws one part's arguments, and reference() takes and returns one part's arrays. A program takes and returns all parts, laid end to end along the dimension named above; an argument that names none is the same for every part. Nothing has to cross between parts.
Inputs may be any that keep to these rules, and one draw needn't show every extreme that they name: `band_start`: A multiple of 128. For a slice of group g (slices 16 * g to 16 * (g + 1) - 1) it is 128 * (g - 1) or 128 * g, never negative. `band_len`: A multiple of 128. The band of a slice of group g covers detector rows 128 * g to 128 * (g + 1) - 1 and ends at or before row 128 * (g + 2) and at or before row 512.
All inputs are finite; a program needn't handle non-finite values.
Results may differ from the reference program's by a relative error of at most 0.0046.
Values may be sent and summed in bfloat16 or wider, within the bound.
A program may use at most 64 MiB of HBM per device.

```python
import math
import jax
import jax.numpy as jnp
from jax import lax

NY = 512
Z_DEV = 16
DC = 2048
BLK = 128
NV = 2
NX = 512
NZ = 64
DR = 512
WIN = 384


def band_choice(key):
    groups = NZ // Z_DEV
    slab_index = jnp.arange(NZ, dtype=jnp.int32)
    group_index = slab_index // Z_DEV
    inside = slab_index % Z_DEV
    distance = jnp.abs(2 * group_index + 1 - groups)
    lower_draw = jax.random.randint(jax.random.fold_in(key, 11), (NV, NZ), 0, 2 * groups)
    upper_draw = jax.random.randint(jax.random.fold_in(key, 12), (NV, NZ), 0, 2 * groups)
    extend_lower = (lower_draw < distance[None, :] + groups // 2) & (group_index[None, :] > 0)
    extend_upper = (upper_draw < distance[None, :] + groups // 2) & (group_index[None, :] < groups - 1)
    longest = (inside == 0) & (group_index == 1)
    shortest = (inside == 0) & (group_index == groups // 2)
    topmost = (inside == 0) & (group_index == groups - 1)
    extend_lower = (extend_lower | longest[None, :]) & ~shortest[None, :] & ~topmost[None, :]
    extend_upper = (extend_upper | longest[None, :]) & ~shortest[None, :]
    lower_count = extend_lower.astype(jnp.int32)
    upper_count = extend_upper.astype(jnp.int32)
    first_rows = (group_index[None, :] - lower_count) * BLK
    row_counts = (1 + lower_count + upper_count) * BLK
    return (first_rows.astype(jnp.int32), row_counts.astype(jnp.int32))


def draw_band_start(key, part):
    first_rows, row_counts = band_choice(key)
    return first_rows


def draw_band_len(key, part):
    first_rows, row_counts = band_choice(key)
    return row_counts


def shard_levels(rng, extent, split, least, top_value):
    gain, own = 1.0, jax.random.fold_in(rng, 6)
    for axis_at, blocks in split:
        draws = jnp.exp(jax.random.uniform(jax.random.fold_in(own, axis_at), (blocks,), jnp.float32, least / len(split), top_value / len(split)))
        gain = gain * jnp.repeat(draws, extent[axis_at] // blocks).reshape([-1 if axis == axis_at else 1 for axis in range(len(extent))])
    return gain


def centred(own_key, dims, width, most, cuts=(), held_as=jnp.bfloat16):
    loudness = shard_levels(own_key, dims, cuts, -0.22, 0.18) if cuts else 1.0
    drawn = jax.random.normal(own_key, dims, jnp.float32) * width * loudness
    return jnp.minimum(jnp.maximum(drawn, -most), most).astype(held_as)


def setup_inputs(seed: int = 0, part: int = 0) -> dict:
    key_of = jax.random.split(jax.random.key(seed), 9)
    part_splits = jax.random.split(jax.random.fold_in(key_of[8], part), 9)
    return {
        "volume": centred(part_splits[0], (NZ, NX, NY), 1.0, 6.0, ((0, 4), (1, 4)), jnp.float32),
        "col_weight": jnp.clip(jnp.exp(math.log(2.0) - 1.3862944 * jax.random.uniform(key_of[1], (NZ, NX, NY), jnp.float32) ** shard_levels(key_of[1], (NZ, NX, NY), ((0, 4), (1, 4)), -0.2, 0.2)), 0.5, 2.0).astype(jnp.bfloat16),
        "column_map": centred(key_of[2], (NV, NX, DC), NX ** -0.5, 0.25, ((1, 4),)),
        "depth_map": centred(key_of[3], (NV, NY, WIN), (NY * Z_DEV) ** -0.5, 0.0625),
        "measured": centred(part_splits[4], (DC, NV, DR), 1.0, 6.0, ((0, 4), (2, 4)), jnp.float32),
        "row_weight": jnp.clip(jnp.exp(math.log(2.0) - 1.3862944 * jax.random.uniform(key_of[5], (DC, NV, DR), jnp.float32) ** shard_levels(key_of[5], (DC, NV, DR), ((0, 4), (2, 4)), -0.2, 0.2)), 0.5, 2.0),
        "band_start": draw_band_start(jax.random.fold_in(key_of[8], 71), part),
        "band_len": draw_band_len(jax.random.fold_in(key_of[8], 71), part),
    }


def reference(volume, col_weight, column_map, depth_map, measured, row_weight, band_start, band_len):
    groups = NZ // Z_DEV
    coarse = lax.optimization_barrier(volume.astype(jnp.bfloat16)).astype(jnp.float32)
    column_lookup_tables = column_map.astype(jnp.float32)
    depth_maps = depth_map.astype(jnp.float32)
    coarse_groups = coarse.reshape(groups, Z_DEV, NX, NY)
    starts = band_start.reshape(NV, groups, Z_DEV).transpose(1, 0, 2)
    lengths = band_len.reshape(NV, groups, Z_DEV).transpose(1, 0, 2)
    group_ids = jnp.arange(groups, dtype=jnp.int32)
    row_index = jnp.arange(WIN, dtype=jnp.int32)

    def forward(projection, group_items):
        slab_cells, start_rows, length_rows, group_index = group_items
        shifted = (start_rows - (group_index - 1) * BLK) == BLK
        in_band = row_index[None, None, :] < length_rows[:, :, None]
        windows = []
        for which_view in range(NV):
            footprint = jnp.einsum("zxy,yt->zxt", slab_cells, depth_maps[which_view])
            footprint = jnp.where(in_band[which_view][:, None, :], footprint, 0.0)
            first_part = jnp.sum(jnp.where(shifted[which_view][:, None, None], 0.0, footprint), axis=0)
            second_part = jnp.sum(jnp.where(shifted[which_view][:, None, None], footprint, 0.0), axis=0)
            second_part = jnp.concatenate([jnp.zeros((NX, BLK), jnp.float32), second_part[:, :WIN - BLK]], axis=1)
            windows.append(first_part + second_part)
        detector_frame = lax.optimization_barrier(jnp.stack(windows).astype(jnp.bfloat16)).astype(jnp.float32)
        incomplete_sum = jnp.einsum("piu,pit->upt", column_lookup_tables, detector_frame)
        first_row = (group_index * BLK).astype(jnp.int32)
        current = lax.dynamic_slice_in_dim(projection, first_row, WIN, 2)
        projection = lax.dynamic_update_slice_in_dim(projection, current + incomplete_sum, first_row, 2)
        return projection, None

    projection, _ = lax.scan(forward, jnp.zeros((DC, NV, DR + 2 * BLK), jnp.float32),
                             (coarse_groups, starts, lengths, group_ids))
    projection = projection[:, :, BLK:BLK + DR]
    residual = (row_weight * (measured - projection)).astype(jnp.bfloat16)
    residual = lax.optimization_barrier(residual).astype(jnp.float32)
    edge_rows = jnp.zeros((DC, NV, BLK), jnp.float32)
    padded = jnp.concatenate([edge_rows, residual, edge_rows], axis=2)

    def backward(group_items):
        start_rows, length_rows, group_index = group_items
        shifted = (start_rows - (group_index - 1) * BLK) == BLK
        in_band = row_index[None, None, :] < length_rows[:, :, None]
        first_row = (group_index * BLK).astype(jnp.int32)
        frame_rows = lax.dynamic_slice_in_dim(padded, first_row, WIN, 2)
        distribute_rays = jnp.einsum("phr,rpk->phk", column_lookup_tables, frame_rows).astype(jnp.bfloat16)
        distribute_rays = lax.optimization_barrier(distribute_rays).astype(jnp.float32)
        result = jnp.zeros((Z_DEV, NX, NY), jnp.float32)
        for which_view in range(NV):
            advanced = jnp.concatenate([distribute_rays[which_view][:, BLK:], jnp.zeros((NX, BLK), jnp.float32)], axis=1)
            chosen = jnp.where(shifted[which_view][:, None, None], advanced[None], distribute_rays[which_view][None])
            chosen = jnp.where(in_band[which_view][:, None, :], chosen, 0.0)
            result = result + jnp.einsum("zxt,yt->zxy", chosen, depth_maps[which_view])
        return result

    backprojected = lax.map(backward, (starts, lengths, group_ids)).reshape(NZ, NX, NY)
    return volume + col_weight.astype(jnp.float32) * backprojected
```

```python
import functools

import jax
import jax.numpy as jnp
from jax import lax
from jax.experimental import pallas as pl
from jax.experimental.pallas import tpu as pltpu
from jax.sharding import PartitionSpec as P

BLK = 128
VIEWS = 2
CHUNK = 4
MESH = pl.DeviceIdType.MESH
BF16 = jnp.bfloat16
F32 = jnp.float32


def middle_kernel(
    n, groups,
    start_ref, len_ref, volume, depth, colmap, measured, weight,
    out_ref,
    vol, dcat, maps, meas, rw, meas_t, rw_t, acc, wt, halo, gathered, part, parts_in, own, halo_s,
    vol_sem, dep_sem, loc_sem,
    m_send, m_recv, f_send, f_recv, h_send, h_recv, g_send, g_recv, r_send, r_recv, s_send, s_recv,
):
    g = lax.axis_index("gz")
    me = lax.axis_index("gx")
    core = lax.rem(g, 2)
    sibling = g + 1 - 2 * core
    cols = maps.shape[2]
    slices = vol.shape[0]
    steps = slices // CHUNK
    t_len = depth.shape[2]

    def my_columns(who):
        return pl.ds(pl.multiple_of(who * cols, 128), cols)

    def x_rows(who):
        return pl.ds(pl.multiple_of(who * BLK, BLK), BLK)

    depth_copies = [
        pltpu.make_async_copy(depth.at[v], dcat.at[:, pl.ds(v * t_len, t_len)], dep_sem.at[v])
        for v in range(VIEWS)
    ]
    for copy in depth_copies:
        copy.start()

    def vol_copy(k):
        return pltpu.make_async_copy(
            volume.at[pl.ds(k * CHUNK, CHUNK)], vol.at[pl.ds(k * CHUNK, CHUNK)], vol_sem.at[k]
        )

    for k in range(steps):
        vol_copy(k).start()
    local_copies = [
        pltpu.make_async_copy(colmap.at[:, :, my_columns(me)], maps.at[:, x_rows(me), :], loc_sem.at[0]),
        pltpu.make_async_copy(measured, meas, loc_sem.at[1]),
        pltpu.make_async_copy(weight, rw, loc_sem.at[2]),
    ]
    for copy in local_copies:
        copy.start()

    barrier = pltpu.get_barrier_semaphore()
    for d in range(1, n):
        pl.semaphore_signal(barrier, inc=1, device_id={"gx": lax.rem(me + d, n)}, device_id_type=MESH)

    @pl.when(g > 0)
    def _():
        pl.semaphore_signal(barrier, inc=1, device_id={"gz": g - 1}, device_id_type=MESH)

    @pl.when(g < groups - 1)
    def _():
        pl.semaphore_signal(barrier, inc=1, device_id={"gz": g + 1}, device_id_type=MESH)

    below = jnp.where(g > 0, 1, 0)
    above = jnp.where(g < groups - 1, 1, 0)
    pl.semaphore_wait(barrier, n - 1 + below + above)

    def map_copy(d):
        peer = lax.rem(me + d, n)
        return pltpu.make_async_remote_copy(
            src_ref=colmap.at[core, :, my_columns(peer)],
            dst_ref=maps.at[core, x_rows(me), :],
            send_sem=m_send.at[d], recv_sem=m_recv.at[d],
            device_id={"gx": peer}, device_id_type=MESH,
        )

    for d in range(1, n):
        map_copy(d).start()

    acc[...] = jnp.zeros_like(acc)
    for copy in depth_copies:
        copy.wait()

    def forward(k, carry):
        vol_copy(k).wait()
        coarse = vol[pl.ds(k * CHUNK, CHUNK)].astype(BF16).reshape(CHUNK * BLK, vol.shape[2])
        foot = jnp.dot(coarse, dcat[...], preferred_element_type=F32)
        for v in range(VIEWS):
            sums = [acc[v, b] for b in range(3)]
            for i in range(CHUNK):
                z = k * CHUNK + i
                low = jnp.where(start_ref[v, z] < g * BLK, 1.0, 0.0).astype(F32)
                up = jnp.where(start_ref[v, z] + len_ref[v, z] > (g + 1) * BLK, 1.0, 0.0).astype(F32)
                t = [
                    foot[i * BLK:(i + 1) * BLK, v * t_len + b * BLK:v * t_len + (b + 1) * BLK]
                    for b in range(3)
                ]
                sums[0] = sums[0] + low * t[0]
                sums[1] = sums[1] + low * t[1] + (1.0 - low) * t[0]
                sums[2] = sums[2] + (low * up) * t[2] + ((1.0 - low) * up) * t[1]
            for b in range(3):
                acc[v, b] = sums[b]
        return carry

    lax.fori_loop(0, steps, forward, 0)
    for b in (0, 2):
        for v in range(VIEWS):
            wt[b // 2, v] = acc[v, b].T.astype(BF16)

    def to_below(src, dst, send, recv):
        return pltpu.make_async_remote_copy(
            src_ref=src, dst_ref=dst, send_sem=send.at[0], recv_sem=recv.at[0],
            device_id={"gz": g - 1}, device_id_type=MESH,
        )

    def to_above(src, dst, send, recv):
        return pltpu.make_async_remote_copy(
            src_ref=src, dst_ref=dst, send_sem=send.at[1], recv_sem=recv.at[1],
            device_id={"gz": g + 1}, device_id_type=MESH,
        )

    def exchange_start(low_src, high_src, land, send, recv):
        @pl.when(g > 0)
        def _():
            to_below(low_src, land.at[1], send, recv).start()

        @pl.when(g < groups - 1)
        def _():
            to_above(high_src, land.at[0], send, recv).start()

        @pl.when(g == 0)
        def _():
            land[0] = jnp.zeros_like(land[0])

        @pl.when(g == groups - 1)
        def _():
            land[1] = jnp.zeros_like(land[1])

    def exchange_wait(low_src, high_src, land, send, recv):
        @pl.when(g > 0)
        def _():
            to_below(low_src, land.at[1], send, recv).wait_send()
            to_above(high_src, land.at[0], send, recv).wait_recv()

        @pl.when(g < groups - 1)
        def _():
            to_above(high_src, land.at[0], send, recv).wait_send()
            to_below(low_src, land.at[1], send, recv).wait_recv()

    exchange_start(wt.at[0], wt.at[1], halo, h_send, h_recv)
    for copy in local_copies:
        copy.wait()
    for v in range(VIEWS):
        meas_t[v] = meas[pl.ds(v, cols, stride=VIEWS), :].T
        rw_t[v] = rw[pl.ds(v, cols, stride=VIEWS), :].T
    middle = [acc[v, 1].T.astype(BF16).astype(F32) for v in range(VIEWS)]
    exchange_wait(wt.at[0], wt.at[1], halo, h_send, h_recv)
    for v in range(VIEWS):
        total = middle[v] + halo[0, v].astype(F32) + halo[1, v].astype(F32)
        gathered[me, v] = total.astype(BF16)

    def gather_copy(d, slot):
        return pltpu.make_async_remote_copy(
            src_ref=gathered.at[slot], dst_ref=gathered.at[slot],
            send_sem=g_send.at[d], recv_sem=g_recv.at[d],
            device_id={"gx": lax.rem(me + d, n)}, device_id_type=MESH,
        )

    for d in range(1, n):
        gather_copy(d, me).start()

    def forward_copy(d, view):
        src = lax.rem(me - d + n, n)
        return pltpu.make_async_remote_copy(
            src_ref=maps.at[view, x_rows(src), :], dst_ref=maps.at[view, x_rows(src), :],
            send_sem=f_send.at[d], recv_sem=f_recv.at[d],
            device_id={"gz": sibling}, device_id_type=MESH,
        )

    for d in range(1, n):
        map_copy(d).wait_recv()
        forward_copy(d, core).start()
    for d in range(1, n):
        gather_copy(d, lax.rem(me - d + n, n)).wait_recv()
    for d in range(1, n):
        forward_copy(d, 1 - core).wait_recv()

    own_parts = []
    for v in range(VIEWS):
        window = jnp.concatenate([gathered[j, v] for j in range(n)], axis=1)
        projection = jnp.dot(window, maps[v], preferred_element_type=F32)
        residual = (rw_t[v] * (meas_t[v] - projection)).astype(BF16)
        spread = lax.dot_general(residual, maps[v], (((1,), (1,)), ((), ())), preferred_element_type=F32)
        for j in range(n):
            own[j, v] = spread[:, j * BLK:(j + 1) * BLK]
            part[j, v] = spread[:, j * BLK:(j + 1) * BLK].astype(BF16)

    def reduce_copy(d):
        peer = lax.rem(me + d, n)
        return pltpu.make_async_remote_copy(
            src_ref=part.at[peer], dst_ref=parts_in.at[d],
            send_sem=r_send.at[d], recv_sem=r_recv.at[d],
            device_id={"gx": peer}, device_id_type=MESH,
        )

    for d in range(1, n):
        reduce_copy(d).start()
    totals = [own[me, v] for v in range(VIEWS)]
    for d in range(1, n):
        reduce_copy(d).wait_recv()
        totals = [totals[v] + parts_in[d, v].astype(F32) for v in range(VIEWS)]
    for v in range(VIEWS):
        halo_s[2, v] = totals[v].T.astype(BF16)

    exchange_start(halo_s.at[2], halo_s.at[2], halo_s, s_send, s_recv)
    out_ref[1] = halo_s[2]
    exchange_wait(halo_s.at[2], halo_s.at[2], halo_s, s_send, s_recv)
    out_ref[0] = halo_s[0]
    out_ref[2] = halo_s[1]
    for d in range(1, n):
        map_copy(d).wait_send()
        gather_copy(d, me).wait_send()
        forward_copy(d, core).wait_send()
        reduce_copy(d).wait_send()


def middle(volume, column_map, depth_map, measured, row_weight, band_start, band_len):
    n, groups = lax.axis_size("gx"), lax.axis_size("gz")
    slices, x_columns, y_cells = volume.shape
    views, _, t_len = depth_map.shape
    cols = measured.shape[0]
    hbm = pl.BlockSpec(memory_space=pl.ANY)
    smem = pl.BlockSpec(memory_space=pltpu.SMEM)
    block = (views, BLK, BLK)
    dma = pltpu.SemaphoreType.DMA
    return pl.pallas_call(
        functools.partial(middle_kernel, n, groups),
        out_shape=jax.ShapeDtypeStruct((3, *block), BF16),
        in_specs=[smem, smem, hbm, hbm, hbm, hbm, hbm],
        out_specs=pl.BlockSpec(memory_space=pltpu.VMEM),
        scratch_shapes=[
            pltpu.VMEM((slices, x_columns, y_cells), F32),
            pltpu.VMEM((y_cells, views * t_len), BF16),
            pltpu.VMEM((views, n * BLK, cols), BF16),
            pltpu.VMEM((cols * views, BLK), F32),
            pltpu.VMEM((cols * views, BLK), F32),
            pltpu.VMEM((views, BLK, cols), F32),
            pltpu.VMEM((views, BLK, cols), F32),
            pltpu.VMEM((views, 3, BLK, BLK), F32),
            pltpu.VMEM((2, *block), BF16),
            pltpu.VMEM((2, *block), BF16),
            pltpu.VMEM((n, *block), BF16),
            pltpu.VMEM((n, *block), BF16),
            pltpu.VMEM((n, *block), BF16),
            pltpu.VMEM((n, *block), F32),
            pltpu.VMEM((3, *block), BF16),
            dma((slices // CHUNK,)), dma((views,)), dma((3,)),
            dma((n,)), dma((n,)), dma((n,)), dma((n,)), dma((2,)), dma((2,)),
            dma((n,)), dma((n,)), dma((n,)), dma((n,)), dma((2,)), dma((2,)),
        ],
        compiler_params=pltpu.CompilerParams(
            collective_id=0, has_side_effects=True, vmem_limit_bytes=32 * 1024 * 1024
        ),
        name="project_and_spread",
    )(
        band_start, band_len, volume, depth_map, column_map,
        measured.reshape(cols * views, BLK), row_weight.reshape(cols * views, BLK),
    )


def back_kernel(start_ref, len_ref, spread, depth, volume, col_weight, out_ref, images):
    g = lax.axis_index("gz")
    step = pl.program_id(0)
    depth_contract = (((1,), (1,)), ((), ()))

    @pl.when(step == 0)
    def _():
        for v in range(VIEWS):
            low = jnp.concatenate([spread[0, v], spread[1, v]], axis=1)
            high = jnp.concatenate([spread[1, v], spread[2, v]], axis=1)
            pair = lax.dot_general(
                jnp.concatenate([low, high], axis=0), depth[v, :, :2 * BLK],
                depth_contract, preferred_element_type=F32,
            )
            images[v, 0] = lax.dot_general(
                spread[1, v], depth[v, :, :BLK], depth_contract, preferred_element_type=F32
            )
            images[v, 1] = pair[:BLK]
            images[v, 2] = pair[BLK:]
            images[v, 3] = pair[:BLK] + lax.dot_general(
                spread[2, v], depth[v, :, 2 * BLK:], depth_contract, preferred_element_type=F32
            )

    count = volume.shape[0]
    for i in range(count):
        z = step * count + i
        total = None
        for v in range(VIEWS):
            low = (start_ref[v, z] < g * BLK).astype(jnp.int32)
            up = (start_ref[v, z] + len_ref[v, z] > (g + 1) * BLK).astype(jnp.int32)
            image = images[v, low + 2 * up]
            total = image if total is None else total + image
        out_ref[i] = volume[i] + col_weight[i].astype(F32) * total


def back(spread, depth_map, volume, col_weight, band_start, band_len):
    slices, x_columns, y_cells = volume.shape
    count = 2
    smem = pl.BlockSpec(memory_space=pltpu.SMEM)
    slab = pl.BlockSpec((count, x_columns, y_cells), lambda i: (i, 0, 0))
    return pl.pallas_call(
        back_kernel,
        grid=(slices // count,),
        out_shape=jax.ShapeDtypeStruct(volume.shape, F32),
        in_specs=[
            smem, smem,
            pl.BlockSpec(spread.shape, lambda i: (0, 0, 0, 0)),
            pl.BlockSpec(depth_map.shape, lambda i: (0, 0, 0)),
            slab, slab,
        ],
        out_specs=slab,
        scratch_shapes=[pltpu.VMEM((VIEWS, 4, x_columns, y_cells), F32)],
        compiler_params=pltpu.CompilerParams(vmem_limit_bytes=32 * 1024 * 1024),
        name="backproject",
    )(band_start, band_len, spread, depth_map, volume, col_weight)


def local(volume, col_weight, column_map, depth_map, measured, row_weight, band_start, band_len):
    spread = middle(volume, column_map, depth_map, measured, row_weight, band_start, band_len)
    return back(spread, depth_map, volume, col_weight, band_start, band_len)


def solution(mesh):
    in_specs = (
        P(("grp", "gz"), "gx", None),
        P("gz", "gx", None),
        P(None, "gx", None),
        P(),
        P(("grp", "gx"), None, "gz"),
        P("gx", None, "gz"),
        P(None, "gz"),
        P(None, "gz"),
    )
    out_specs = P(("grp", "gz"), "gx", None)
    return jax.shard_map(local, mesh=mesh, in_specs=in_specs, out_specs=out_specs, check_vma=False)
```

```python
import functools

import jax
import jax.numpy as jnp
from jax import lax
from jax.experimental import pallas as pl
from jax.experimental.pallas import tpu as pltpu
from jax.sharding import PartitionSpec as P

BLK = 128
VIEWS = 2
CHUNK = 4
GRANT = 64 * 1024 * 1024 - 64 * 1024
MESH = pl.DeviceIdType.MESH
BF16 = jnp.bfloat16
F32 = jnp.float32


def middle_kernel(
    n, groups,
    starts, lens, volume, depth, colmap, measured, weight,
    out_ref,
    start_ref, len_ref, vol, dcat, maps, meas, rw, meas_t, rw_t, acc, wt, halo, gathered, part, parts_in, own, halo_s,
    vol_sem, dep_sem, loc_sem,
    m_send, m_recv, f_send, f_recv, h_send, h_recv, g_send, g_recv, r_send, r_recv, s_send, s_recv,
):
    g = lax.axis_index("gz")
    me = lax.axis_index("gx")
    core = lax.rem(g, 2)
    sibling = g + 1 - 2 * core
    cols = maps.shape[2]
    slices = vol.shape[0]
    steps = slices // CHUNK
    t_len = depth.shape[2]

    def my_columns(who):
        return pl.ds(pl.multiple_of(who * cols, 128), cols)

    def x_rows(who):
        return pl.ds(pl.multiple_of(who * BLK, BLK), BLK)

    depth_copies = [
        pltpu.make_async_copy(depth.at[v], dcat.at[:, pl.ds(v * t_len, t_len)], dep_sem.at[v])
        for v in range(VIEWS)
    ]
    for copy in depth_copies:
        copy.start()

    def vol_copy(k):
        return pltpu.make_async_copy(
            volume.at[pl.ds(k * CHUNK, CHUNK)], vol.at[pl.ds(k * CHUNK, CHUNK)], vol_sem.at[k]
        )

    for k in range(steps):
        vol_copy(k).start()
    band_copies = [
        pltpu.make_async_copy(starts, start_ref, loc_sem.at[3]),
        pltpu.make_async_copy(lens, len_ref, loc_sem.at[4]),
    ]
    for copy in band_copies:
        copy.start()
    local_copies = [
        pltpu.make_async_copy(colmap.at[:, :, my_columns(me)], maps.at[:, x_rows(me), :], loc_sem.at[0]),
        pltpu.make_async_copy(measured, meas, loc_sem.at[1]),
        pltpu.make_async_copy(weight, rw, loc_sem.at[2]),
    ]
    for copy in local_copies:
        copy.start()

    barrier = pltpu.get_barrier_semaphore()
    for d in range(1, n):
        pl.semaphore_signal(barrier, inc=1, device_id={"gx": lax.rem(me + d, n)}, device_id_type=MESH)

    @pl.when(g > 0)
    def _():
        pl.semaphore_signal(barrier, inc=1, device_id={"gz": g - 1}, device_id_type=MESH)

    @pl.when(g < groups - 1)
    def _():
        pl.semaphore_signal(barrier, inc=1, device_id={"gz": g + 1}, device_id_type=MESH)

    below = jnp.where(g > 0, 1, 0)
    above = jnp.where(g < groups - 1, 1, 0)
    pl.semaphore_wait(barrier, n - 1 + below + above)

    def map_copy(d):
        peer = lax.rem(me + d, n)
        return pltpu.make_async_remote_copy(
            src_ref=colmap.at[core, :, my_columns(peer)],
            dst_ref=maps.at[core, x_rows(me), :],
            send_sem=m_send.at[d], recv_sem=m_recv.at[d],
            device_id={"gx": peer}, device_id_type=MESH,
        )

    for d in range(1, n):
        map_copy(d).start()

    acc[...] = jnp.zeros_like(acc)
    for copy in depth_copies + band_copies:
        copy.wait()

    def forward(k, carry):
        vol_copy(k).wait()
        coarse = vol[pl.ds(k * CHUNK, CHUNK)].astype(BF16).reshape(CHUNK * BLK, vol.shape[2])
        foot = jnp.dot(coarse, dcat[...], preferred_element_type=F32)
        for v in range(VIEWS):
            sums = [acc[v, b] for b in range(3)]
            for i in range(CHUNK):
                z = k * CHUNK + i
                low = jnp.where(start_ref[v, z] < g * BLK, 1.0, 0.0).astype(F32)
                up = jnp.where(start_ref[v, z] + len_ref[v, z] > (g + 1) * BLK, 1.0, 0.0).astype(F32)
                t = [
                    foot[i * BLK:(i + 1) * BLK, v * t_len + b * BLK:v * t_len + (b + 1) * BLK]
                    for b in range(3)
                ]
                sums[0] = sums[0] + low * t[0]
                sums[1] = sums[1] + low * t[1] + (1.0 - low) * t[0]
                sums[2] = sums[2] + (low * up) * t[2] + ((1.0 - low) * up) * t[1]
            for b in range(3):
                acc[v, b] = sums[b]
        return carry

    lax.fori_loop(0, steps, forward, 0)
    for b in (0, 2):
        for v in range(VIEWS):
            wt[b // 2, v] = acc[v, b].T.astype(BF16)

    def to_below(src, dst, send, recv):
        return pltpu.make_async_remote_copy(
            src_ref=src, dst_ref=dst, send_sem=send.at[0], recv_sem=recv.at[0],
            device_id={"gz": g - 1}, device_id_type=MESH,
        )

    def to_above(src, dst, send, recv):
        return pltpu.make_async_remote_copy(
            src_ref=src, dst_ref=dst, send_sem=send.at[1], recv_sem=recv.at[1],
            device_id={"gz": g + 1}, device_id_type=MESH,
        )

    def exchange_start(low_src, high_src, land, send, recv):
        @pl.when(g > 0)
        def _():
            to_below(low_src, land.at[1], send, recv).start()

        @pl.when(g < groups - 1)
        def _():
            to_above(high_src, land.at[0], send, recv).start()

        @pl.when(g == 0)
        def _():
            land[0] = jnp.zeros_like(land[0])

        @pl.when(g == groups - 1)
        def _():
            land[1] = jnp.zeros_like(land[1])

    def exchange_wait(low_src, high_src, land, send, recv):
        @pl.when(g > 0)
        def _():
            to_below(low_src, land.at[1], send, recv).wait_send()
            to_above(high_src, land.at[0], send, recv).wait_recv()

        @pl.when(g < groups - 1)
        def _():
            to_above(high_src, land.at[0], send, recv).wait_send()
            to_below(low_src, land.at[1], send, recv).wait_recv()

    exchange_start(wt.at[0], wt.at[1], halo, h_send, h_recv)
    for copy in local_copies:
        copy.wait()
    for v in range(VIEWS):
        meas_t[v] = meas[pl.ds(v, cols, stride=VIEWS), :].T
        rw_t[v] = rw[pl.ds(v, cols, stride=VIEWS), :].T
    middle = [acc[v, 1].T.astype(BF16).astype(F32) for v in range(VIEWS)]
    exchange_wait(wt.at[0], wt.at[1], halo, h_send, h_recv)
    for v in range(VIEWS):
        total = middle[v] + halo[0, v].astype(F32) + halo[1, v].astype(F32)
        gathered[me, v] = total.astype(BF16)

    def gather_copy(d, slot):
        return pltpu.make_async_remote_copy(
            src_ref=gathered.at[slot], dst_ref=gathered.at[slot],
            send_sem=g_send.at[d], recv_sem=g_recv.at[d],
            device_id={"gx": lax.rem(me + d, n)}, device_id_type=MESH,
        )

    for d in range(1, n):
        gather_copy(d, me).start()

    def forward_copy(d, view):
        src = lax.rem(me - d + n, n)
        return pltpu.make_async_remote_copy(
            src_ref=maps.at[view, x_rows(src), :], dst_ref=maps.at[view, x_rows(src), :],
            send_sem=f_send.at[d], recv_sem=f_recv.at[d],
            device_id={"gz": sibling}, device_id_type=MESH,
        )

    for d in range(1, n):
        map_copy(d).wait_recv()
        forward_copy(d, core).start()
    for d in range(1, n):
        gather_copy(d, lax.rem(me - d + n, n)).wait_recv()
    for d in range(1, n):
        forward_copy(d, 1 - core).wait_recv()

    own_parts = []
    for v in range(VIEWS):
        window = jnp.concatenate([gathered[j, v] for j in range(n)], axis=1)
        projection = jnp.dot(window, maps[v], preferred_element_type=F32)
        residual = (rw_t[v] * (meas_t[v] - projection)).astype(BF16)
        spread = lax.dot_general(residual, maps[v], (((1,), (1,)), ((), ())), preferred_element_type=F32)
        for j in range(n):
            own[j, v] = spread[:, j * BLK:(j + 1) * BLK]
            part[j, v] = spread[:, j * BLK:(j + 1) * BLK].astype(BF16)

    def reduce_copy(d):
        peer = lax.rem(me + d, n)
        return pltpu.make_async_remote_copy(
            src_ref=part.at[peer], dst_ref=parts_in.at[d],
            send_sem=r_send.at[d], recv_sem=r_recv.at[d],
            device_id={"gx": peer}, device_id_type=MESH,
        )

    for d in range(1, n):
        reduce_copy(d).start()
    totals = [own[me, v] for v in range(VIEWS)]
    for d in range(1, n):
        reduce_copy(d).wait_recv()
        totals = [totals[v] + parts_in[d, v].astype(F32) for v in range(VIEWS)]
    for v in range(VIEWS):
        halo_s[2, v] = totals[v].T.astype(BF16)

    exchange_start(halo_s.at[2], halo_s.at[2], halo_s, s_send, s_recv)
    out_ref[1] = halo_s[2]
    exchange_wait(halo_s.at[2], halo_s.at[2], halo_s, s_send, s_recv)
    out_ref[0] = halo_s[0]
    out_ref[2] = halo_s[1]
    for d in range(1, n):
        map_copy(d).wait_send()
        gather_copy(d, me).wait_send()
        forward_copy(d, core).wait_send()
        reduce_copy(d).wait_send()


def middle(volume, column_map, depth_map, measured, row_weight, band_start, band_len):
    n, groups = lax.axis_size("gx"), lax.axis_size("gz")
    slices, x_columns, y_cells = volume.shape
    views, _, t_len = depth_map.shape
    cols = measured.shape[0]
    hbm = pl.BlockSpec(memory_space=pl.ANY)
    block = (views, BLK, BLK)
    dma = pltpu.SemaphoreType.DMA
    return pl.pallas_call(
        functools.partial(middle_kernel, n, groups),
        out_shape=jax.ShapeDtypeStruct((3, *block), BF16),
        in_specs=[hbm] * 7,
        out_specs=pl.BlockSpec(memory_space=pltpu.VMEM),
        scratch_shapes=[
            pltpu.SMEM((views, slices), jnp.int32),
            pltpu.SMEM((views, slices), jnp.int32),
            pltpu.VMEM((slices, x_columns, y_cells), F32),
            pltpu.VMEM((y_cells, views * t_len), BF16),
            pltpu.VMEM((views, n * BLK, cols), BF16),
            pltpu.VMEM((cols * views, BLK), F32),
            pltpu.VMEM((cols * views, BLK), F32),
            pltpu.VMEM((views, BLK, cols), F32),
            pltpu.VMEM((views, BLK, cols), F32),
            pltpu.VMEM((views, 3, BLK, BLK), F32),
            pltpu.VMEM((2, *block), BF16),
            pltpu.VMEM((2, *block), BF16),
            pltpu.VMEM((n, *block), BF16),
            pltpu.VMEM((n, *block), BF16),
            pltpu.VMEM((n, *block), BF16),
            pltpu.VMEM((n, *block), F32),
            pltpu.VMEM((3, *block), BF16),
            dma((slices // CHUNK,)), dma((views,)), dma((5,)),
            dma((n,)), dma((n,)), dma((n,)), dma((n,)), dma((2,)), dma((2,)),
            dma((n,)), dma((n,)), dma((n,)), dma((n,)), dma((2,)), dma((2,)),
        ],
        compiler_params=pltpu.CompilerParams(
            collective_id=0, has_side_effects=True, vmem_limit_bytes=GRANT
        ),
        name="project_and_spread",
    )(
        band_start, band_len, volume, depth_map, column_map,
        measured.reshape(cols * views, BLK), row_weight.reshape(cols * views, BLK),
    )


def back_kernel(
    starts, lens, spread_in, depth_in, volume, col_weight, out,
    start_ref, len_ref, spread, depth, vol, cw, images, result,
    in_sem, vol_sem, cw_sem, out_sem,
):
    g = lax.axis_index("gz")
    slices = vol.shape[0]
    first_copies = [
        pltpu.make_async_copy(spread_in, spread, in_sem.at[0]),
        pltpu.make_async_copy(depth_in, depth, in_sem.at[1]),
        pltpu.make_async_copy(starts, start_ref, in_sem.at[2]),
        pltpu.make_async_copy(lens, len_ref, in_sem.at[3]),
    ]
    for copy in first_copies:
        copy.start()

    def part(ref, k):
        return ref.at[pl.ds(k * CHUNK, CHUNK)]

    def vol_copy(k):
        return pltpu.make_async_copy(part(volume, k), part(vol, k), vol_sem.at[k])

    def cw_copy(k):
        return pltpu.make_async_copy(part(col_weight, k), part(cw, k), cw_sem.at[k])

    for k in range(slices // CHUNK):
        vol_copy(k).start()
        cw_copy(k).start()
    for copy in first_copies:
        copy.wait()
    depth_contract = (((1,), (1,)), ((), ()))
    for v in range(VIEWS):
        low = jnp.concatenate([spread[0, v], spread[1, v]], axis=1)
        high = jnp.concatenate([spread[1, v], spread[2, v]], axis=1)
        pair = lax.dot_general(
            jnp.concatenate([low, high], axis=0), depth[v, :, :2 * BLK],
            depth_contract, preferred_element_type=F32,
        )
        images[v, 0] = lax.dot_general(
            spread[1, v], depth[v, :, :BLK], depth_contract, preferred_element_type=F32
        )
        images[v, 1] = pair[:BLK]
        images[v, 2] = pair[BLK:]
        images[v, 3] = pair[:BLK] + lax.dot_general(
            spread[2, v], depth[v, :, 2 * BLK:], depth_contract, preferred_element_type=F32
        )

    def out_copy(z):
        return pltpu.make_async_copy(result.at[z], out.at[z], out_sem.at[z])

    def update(k, carry):
        vol_copy(k).wait()
        cw_copy(k).wait()
        for i in range(CHUNK):
            z = k * CHUNK + i
            total = None
            for v in range(VIEWS):
                low = (start_ref[v, z] < g * BLK).astype(jnp.int32)
                up = (start_ref[v, z] + len_ref[v, z] > (g + 1) * BLK).astype(jnp.int32)
                image = images[v, low + 2 * up]
                total = image if total is None else total + image
            result[z] = vol[z] + cw[z].astype(F32) * total
            out_copy(z).start()
        return carry

    lax.fori_loop(0, slices // CHUNK, update, 0)
    for z in range(slices):
        out_copy(z).wait()


def back(spread, depth_map, volume, col_weight, band_start, band_len):
    slices, x_columns, y_cells = volume.shape
    hbm = pl.BlockSpec(memory_space=pl.ANY)
    dma = pltpu.SemaphoreType.DMA
    return pl.pallas_call(
        back_kernel,
        out_shape=jax.ShapeDtypeStruct(volume.shape, F32),
        in_specs=[hbm] * 6,
        out_specs=hbm,
        scratch_shapes=[
            pltpu.SMEM(band_start.shape, jnp.int32),
            pltpu.SMEM(band_start.shape, jnp.int32),
            pltpu.VMEM(spread.shape, BF16),
            pltpu.VMEM(depth_map.shape, BF16),
            pltpu.VMEM(volume.shape, F32),
            pltpu.VMEM(volume.shape, BF16),
            pltpu.VMEM((VIEWS, 4, x_columns, y_cells), F32),
            pltpu.VMEM(volume.shape, F32),
            dma((4,)), dma((slices // CHUNK,)), dma((slices // CHUNK,)), dma((slices,)),
        ],
        compiler_params=pltpu.CompilerParams(vmem_limit_bytes=GRANT),
        name="backproject",
    )(band_start, band_len, spread, depth_map, volume, col_weight)


def local(volume, col_weight, column_map, depth_map, measured, row_weight, band_start, band_len):
    spread = middle(volume, column_map, depth_map, measured, row_weight, band_start, band_len)
    return back(spread, depth_map, volume, col_weight, band_start, band_len)


def solution(mesh):
    in_specs = (
        P(("grp", "gz"), "gx", None),
        P("gz", "gx", None),
        P(None, "gx", None),
        P(),
        P(("grp", "gx"), None, "gz"),
        P("gx", None, "gz"),
        P(None, "gz"),
        P(None, "gz"),
    )
    out_specs = P(("grp", "gz"), "gx", None)
    return jax.shard_map(local, mesh=mesh, in_specs=in_specs, out_specs=out_specs, check_vma=False)
```

```python
import functools

import jax
import jax.numpy as jnp
from jax import lax
from jax.experimental import pallas as pl
from jax.experimental.pallas import tpu as pltpu
from jax.sharding import PartitionSpec as P

BLK = 128
VIEWS = 2
CHUNK = 4
GRANT = 64 * 1024 * 1024 - 64 * 1024
MESH = pl.DeviceIdType.MESH
BF16 = jnp.bfloat16
F32 = jnp.float32


def middle_kernel(
    n, groups,
    starts, lens, volume, depth, colmap, measured, weight,
    out_ref,
    start_ref, len_ref, vol, dcat, maps, meas, rw, meas_t, rw_t, acc, wt, halo, gathered, part, parts_in, own, halo_s,
    vol_sem, dep_sem, loc_sem,
    m_send, m_recv, x_send, x_recv, f_send, f_recv, h_send, h_recv, g_send, g_recv, r_send, r_recv, s_send, s_recv,
):
    g = lax.axis_index("gz")
    me = lax.axis_index("gx")
    core = lax.rem(g, 2)
    sibling = g + 1 - 2 * core
    half = lax.rem(g // 2, 2)
    across = g + 2 - 4 * half
    rows = BLK // 2
    cols = maps.shape[2]
    slices = vol.shape[0]
    steps = slices // CHUNK
    t_len = depth.shape[2]

    def my_columns(who):
        return pl.ds(pl.multiple_of(who * cols, 128), cols)

    def x_rows(who):
        return pl.ds(pl.multiple_of(who * BLK, BLK), BLK)

    depth_copies = [
        pltpu.make_async_copy(depth.at[v], dcat.at[:, pl.ds(v * t_len, t_len)], dep_sem.at[v])
        for v in range(VIEWS)
    ]
    for copy in depth_copies:
        copy.start()

    def vol_copy(k):
        return pltpu.make_async_copy(
            volume.at[pl.ds(k * CHUNK, CHUNK)], vol.at[pl.ds(k * CHUNK, CHUNK)], vol_sem.at[k]
        )

    for k in range(steps):
        vol_copy(k).start()
    band_copies = [
        pltpu.make_async_copy(starts, start_ref, loc_sem.at[3]),
        pltpu.make_async_copy(lens, len_ref, loc_sem.at[4]),
    ]
    for copy in band_copies:
        copy.start()
    local_copies = [
        pltpu.make_async_copy(colmap.at[:, :, my_columns(me)], maps.at[:, x_rows(me), :], loc_sem.at[0]),
        pltpu.make_async_copy(measured, meas, loc_sem.at[1]),
        pltpu.make_async_copy(weight, rw, loc_sem.at[2]),
    ]
    for copy in local_copies:
        copy.start()

    barrier = pltpu.get_barrier_semaphore()
    for d in range(1, n):
        pl.semaphore_signal(barrier, inc=1, device_id={"gx": lax.rem(me + d, n)}, device_id_type=MESH)

    @pl.when(g > 0)
    def _():
        pl.semaphore_signal(barrier, inc=1, device_id={"gz": g - 1}, device_id_type=MESH)

    @pl.when(g < groups - 1)
    def _():
        pl.semaphore_signal(barrier, inc=1, device_id={"gz": g + 1}, device_id_type=MESH)

    pl.semaphore_signal(barrier, inc=1, device_id={"gz": across}, device_id_type=MESH)
    below = jnp.where(g > 0, 1, 0)
    above = jnp.where(g < groups - 1, 1, 0)
    pl.semaphore_wait(barrier, n + below + above)

    def piece(view, who, which):
        return maps.at[view, pl.ds(pl.multiple_of(who * BLK + which * rows, rows), rows), :]

    def map_copy(d):
        peer = lax.rem(me + d, n)
        return pltpu.make_async_remote_copy(
            src_ref=colmap.at[core, pl.ds(pl.multiple_of(half * rows, rows), rows), my_columns(peer)],
            dst_ref=piece(core, me, half),
            send_sem=m_send.at[d], recv_sem=m_recv.at[d],
            device_id={"gx": peer}, device_id_type=MESH,
        )

    def across_copy(d, which):
        src = piece(core, lax.rem(me - d + n, n), which)
        return pltpu.make_async_remote_copy(
            src_ref=src, dst_ref=src,
            send_sem=x_send.at[d], recv_sem=x_recv.at[d],
            device_id={"gz": across}, device_id_type=MESH,
        )

    def forward_copy(d, view, came, which):
        src = piece(view, lax.rem(me - d + n, n), which)
        return pltpu.make_async_remote_copy(
            src_ref=src, dst_ref=src,
            send_sem=f_send.at[came, d], recv_sem=f_recv.at[came, d],
            device_id={"gz": sibling}, device_id_type=MESH,
        )

    for d in range(1, n):
        map_copy(d).start()

    acc[...] = jnp.zeros_like(acc)
    for copy in depth_copies + band_copies:
        copy.wait()

    def forward(k, carry):
        vol_copy(k).wait()
        coarse = vol[pl.ds(k * CHUNK, CHUNK)].astype(BF16).reshape(CHUNK * BLK, vol.shape[2])
        foot = jnp.dot(coarse, dcat[...], preferred_element_type=F32)
        for v in range(VIEWS):
            sums = [acc[v, b] for b in range(3)]
            for i in range(CHUNK):
                z = k * CHUNK + i
                low = jnp.where(start_ref[v, z] < g * BLK, 1.0, 0.0).astype(F32)
                up = jnp.where(start_ref[v, z] + len_ref[v, z] > (g + 1) * BLK, 1.0, 0.0).astype(F32)
                t = [
                    foot[i * BLK:(i + 1) * BLK, v * t_len + b * BLK:v * t_len + (b + 1) * BLK]
                    for b in range(3)
                ]
                sums[0] = sums[0] + low * t[0]
                sums[1] = sums[1] + low * t[1] + (1.0 - low) * t[0]
                sums[2] = sums[2] + (low * up) * t[2] + ((1.0 - low) * up) * t[1]
            for b in range(3):
                acc[v, b] = sums[b]
        return carry

    lax.fori_loop(0, steps, forward, 0)
    for b in (0, 2):
        for v in range(VIEWS):
            wt[b // 2, v] = acc[v, b].T.astype(BF16)

    def to_below(src, land, send, recv, v):
        return pltpu.make_async_remote_copy(
            src_ref=src, dst_ref=land.at[1, v], send_sem=send.at[0, v], recv_sem=recv.at[0, v],
            device_id={"gz": g - 1}, device_id_type=MESH,
        )

    def to_above(src, land, send, recv, v):
        return pltpu.make_async_remote_copy(
            src_ref=src, dst_ref=land.at[0, v], send_sem=send.at[1, v], recv_sem=recv.at[1, v],
            device_id={"gz": g + 1}, device_id_type=MESH,
        )

    def exchange_start(low_src, high_src, land, send, recv, v):
        @pl.when(g > 0)
        def _():
            to_below(low_src, land, send, recv, v).start()

        @pl.when(g < groups - 1)
        def _():
            to_above(high_src, land, send, recv, v).start()

        @pl.when(g == 0)
        def _():
            land[0, v] = jnp.zeros_like(land[0, v])

        @pl.when(g == groups - 1)
        def _():
            land[1, v] = jnp.zeros_like(land[1, v])

    def exchange_wait(low_src, high_src, land, send, recv, v):
        @pl.when(g > 0)
        def _():
            to_below(low_src, land, send, recv, v).wait_send()
            to_above(high_src, land, send, recv, v).wait_recv()

        @pl.when(g < groups - 1)
        def _():
            to_above(high_src, land, send, recv, v).wait_send()
            to_below(low_src, land, send, recv, v).wait_recv()

    for v in range(VIEWS):
        exchange_start(wt.at[0, v], wt.at[1, v], halo, h_send, h_recv, v)
    for d in range(1, n):
        map_copy(d).wait_recv()
        across_copy(d, half).start()
        forward_copy(d, core, 0, half).start()
    for copy in local_copies:
        copy.wait()
    for v in range(VIEWS):
        meas_t[v] = meas[pl.ds(v, cols, stride=VIEWS), :].T
        rw_t[v] = rw[pl.ds(v, cols, stride=VIEWS), :].T
    middle = [acc[v, 1].T.astype(BF16).astype(F32) for v in range(VIEWS)]
    for v in range(VIEWS):
        exchange_wait(wt.at[0, v], wt.at[1, v], halo, h_send, h_recv, v)
        total = middle[v] + halo[0, v].astype(F32) + halo[1, v].astype(F32)
        gathered[me, v] = total.astype(BF16)

    def gather_copy(d, v, slot):
        return pltpu.make_async_remote_copy(
            src_ref=gathered.at[slot, v], dst_ref=gathered.at[slot, v],
            send_sem=g_send.at[v, d], recv_sem=g_recv.at[v, d],
            device_id={"gx": lax.rem(me + d, n)}, device_id_type=MESH,
        )

    for v in range(VIEWS):
        for d in range(1, n):
            gather_copy(d, v, me).start()
    for d in range(1, n):
        across_copy(d, 1 - half).wait_recv()
        forward_copy(d, core, 1, 1 - half).start()

    def reduce_copy(d, v):
        peer = lax.rem(me + d, n)
        return pltpu.make_async_remote_copy(
            src_ref=part.at[peer, v], dst_ref=parts_in.at[d, v],
            send_sem=r_send.at[v, d], recv_sem=r_recv.at[v, d],
            device_id={"gx": peer}, device_id_type=MESH,
        )

    for v in range(VIEWS):
        if v == 0:
            for d in range(1, n):
                forward_copy(d, 1 - core, 0, half).wait_recv()
                forward_copy(d, 1 - core, 1, 1 - half).wait_recv()
        for d in range(1, n):
            gather_copy(d, v, lax.rem(me - d + n, n)).wait_recv()
        window = jnp.concatenate([gathered[j, v] for j in range(n)], axis=1)
        projection = jnp.dot(window, maps[v], preferred_element_type=F32)
        residual = (rw_t[v] * (meas_t[v] - projection)).astype(BF16)
        spread = lax.dot_general(residual, maps[v], (((1,), (1,)), ((), ())), preferred_element_type=F32)
        for j in range(n):
            own[j, v] = spread[:, j * BLK:(j + 1) * BLK]
            part[j, v] = spread[:, j * BLK:(j + 1) * BLK].astype(BF16)
        for d in range(1, n):
            reduce_copy(d, v).start()

    for v in range(VIEWS):
        total = own[me, v]
        for d in range(1, n):
            reduce_copy(d, v).wait_recv()
            total = total + parts_in[d, v].astype(F32)
        halo_s[2, v] = total.T.astype(BF16)
        exchange_start(halo_s.at[2, v], halo_s.at[2, v], halo_s, s_send, s_recv, v)

    out_ref[1] = halo_s[2]
    for v in range(VIEWS):
        exchange_wait(halo_s.at[2, v], halo_s.at[2, v], halo_s, s_send, s_recv, v)
    out_ref[0] = halo_s[0]
    out_ref[2] = halo_s[1]
    for d in range(1, n):
        map_copy(d).wait_send()
        across_copy(d, half).wait_send()
        forward_copy(d, core, 0, half).wait_send()
        forward_copy(d, core, 1, 1 - half).wait_send()
        for v in range(VIEWS):
            gather_copy(d, v, me).wait_send()
            reduce_copy(d, v).wait_send()


def middle(volume, column_map, depth_map, measured, row_weight, band_start, band_len):
    n, groups = lax.axis_size("gx"), lax.axis_size("gz")
    slices, x_columns, y_cells = volume.shape
    views, _, t_len = depth_map.shape
    cols = measured.shape[0]
    hbm = pl.BlockSpec(memory_space=pl.ANY)
    block = (views, BLK, BLK)
    dma = pltpu.SemaphoreType.DMA
    return pl.pallas_call(
        functools.partial(middle_kernel, n, groups),
        out_shape=jax.ShapeDtypeStruct((3, *block), BF16),
        in_specs=[hbm] * 7,
        out_specs=pl.BlockSpec(memory_space=pltpu.VMEM),
        scratch_shapes=[
            pltpu.SMEM((views, slices), jnp.int32),
            pltpu.SMEM((views, slices), jnp.int32),
            pltpu.VMEM((slices, x_columns, y_cells), F32),
            pltpu.VMEM((y_cells, views * t_len), BF16),
            pltpu.VMEM((views, n * BLK, cols), BF16),
            pltpu.VMEM((cols * views, BLK), F32),
            pltpu.VMEM((cols * views, BLK), F32),
            pltpu.VMEM((views, BLK, cols), F32),
            pltpu.VMEM((views, BLK, cols), F32),
            pltpu.VMEM((views, 3, BLK, BLK), F32),
            pltpu.VMEM((2, *block), BF16),
            pltpu.VMEM((2, *block), BF16),
            pltpu.VMEM((n, *block), BF16),
            pltpu.VMEM((n, *block), BF16),
            pltpu.VMEM((n, *block), BF16),
            pltpu.VMEM((n, *block), F32),
            pltpu.VMEM((3, *block), BF16),
            dma((slices // CHUNK,)), dma((views,)), dma((5,)),
            dma((n,)), dma((n,)), dma((n,)), dma((n,)), dma((2, n)), dma((2, n)),
            dma((2, views)), dma((2, views)), dma((views, n)), dma((views, n)),
            dma((views, n)), dma((views, n)), dma((2, views)), dma((2, views)),
        ],
        compiler_params=pltpu.CompilerParams(
            collective_id=0, has_side_effects=True, vmem_limit_bytes=GRANT
        ),
        name="project_and_spread",
    )(
        band_start, band_len, volume, depth_map, column_map,
        measured.reshape(cols * views, BLK), row_weight.reshape(cols * views, BLK),
    )


def back_kernel(
    starts, lens, spread_in, depth_in, volume, col_weight, out,
    start_ref, len_ref, spread, depth, vol, cw, images, result,
    in_sem, vol_sem, cw_sem, out_sem,
):
    g = lax.axis_index("gz")
    slices = vol.shape[0]
    first_copies = [
        pltpu.make_async_copy(spread_in, spread, in_sem.at[0]),
        pltpu.make_async_copy(depth_in, depth, in_sem.at[1]),
        pltpu.make_async_copy(starts, start_ref, in_sem.at[2]),
        pltpu.make_async_copy(lens, len_ref, in_sem.at[3]),
    ]
    for copy in first_copies:
        copy.start()

    def part(ref, k):
        return ref.at[pl.ds(k * CHUNK, CHUNK)]

    def vol_copy(k):
        return pltpu.make_async_copy(part(volume, k), part(vol, k), vol_sem.at[k])

    def cw_copy(k):
        return pltpu.make_async_copy(part(col_weight, k), part(cw, k), cw_sem.at[k])

    for k in range(slices // CHUNK):
        vol_copy(k).start()
        cw_copy(k).start()
    for copy in first_copies:
        copy.wait()
    depth_contract = (((1,), (1,)), ((), ()))
    for v in range(VIEWS):
        low = jnp.concatenate([spread[0, v], spread[1, v]], axis=1)
        high = jnp.concatenate([spread[1, v], spread[2, v]], axis=1)
        pair = lax.dot_general(
            jnp.concatenate([low, high], axis=0), depth[v, :, :2 * BLK],
            depth_contract, preferred_element_type=F32,
        )
        images[v, 0] = lax.dot_general(
            spread[1, v], depth[v, :, :BLK], depth_contract, preferred_element_type=F32
        )
        images[v, 1] = pair[:BLK]
        images[v, 2] = pair[BLK:]
        images[v, 3] = pair[:BLK] + lax.dot_general(
            spread[2, v], depth[v, :, 2 * BLK:], depth_contract, preferred_element_type=F32
        )

    def out_copy(z):
        return pltpu.make_async_copy(result.at[z], out.at[z], out_sem.at[z])

    def update(k, carry):
        vol_copy(k).wait()
        cw_copy(k).wait()
        for i in range(CHUNK):
            z = k * CHUNK + i
            total = None
            for v in range(VIEWS):
                low = (start_ref[v, z] < g * BLK).astype(jnp.int32)
                up = (start_ref[v, z] + len_ref[v, z] > (g + 1) * BLK).astype(jnp.int32)
                image = images[v, low + 2 * up]
                total = image if total is None else total + image
            result[z] = vol[z] + cw[z].astype(F32) * total
            out_copy(z).start()
        return carry

    lax.fori_loop(0, slices // CHUNK, update, 0)
    for z in range(slices):
        out_copy(z).wait()


def back(spread, depth_map, volume, col_weight, band_start, band_len):
    slices, x_columns, y_cells = volume.shape
    hbm = pl.BlockSpec(memory_space=pl.ANY)
    dma = pltpu.SemaphoreType.DMA
    return pl.pallas_call(
        back_kernel,
        out_shape=jax.ShapeDtypeStruct(volume.shape, F32),
        in_specs=[hbm] * 6,
        out_specs=hbm,
        scratch_shapes=[
            pltpu.SMEM(band_start.shape, jnp.int32),
            pltpu.SMEM(band_start.shape, jnp.int32),
            pltpu.VMEM(spread.shape, BF16),
            pltpu.VMEM(depth_map.shape, BF16),
            pltpu.VMEM(volume.shape, F32),
            pltpu.VMEM(volume.shape, BF16),
            pltpu.VMEM((VIEWS, 4, x_columns, y_cells), F32),
            pltpu.VMEM(volume.shape, F32),
            dma((4,)), dma((slices // CHUNK,)), dma((slices // CHUNK,)), dma((slices,)),
        ],
        compiler_params=pltpu.CompilerParams(vmem_limit_bytes=GRANT),
        name="backproject",
    )(band_start, band_len, spread, depth_map, volume, col_weight)


def local(volume, col_weight, column_map, depth_map, measured, row_weight, band_start, band_len):
    spread = middle(volume, column_map, depth_map, measured, row_weight, band_start, band_len)
    return back(spread, depth_map, volume, col_weight, band_start, band_len)


def solution(mesh):
    in_specs = (
        P(("grp", "gz"), "gx", None),
        P("gz", "gx", None),
        P(None, "gx", None),
        P(),
        P(("grp", "gx"), None, "gz"),
        P("gx", None, "gz"),
        P(None, "gz"),
        P(None, "gz"),
    )
    out_specs = P(("grp", "gz"), "gx", None)
    return jax.shard_map(local, mesh=mesh, in_specs=in_specs, out_specs=out_specs, check_vma=False)
```

```python
import functools

import jax
import jax.numpy as jnp
from jax import lax
from jax.experimental import pallas as pl
from jax.experimental.pallas import tpu as pltpu
from jax.sharding import PartitionSpec as P

BLK = 128
VIEWS = 2
CHUNK = 4
GRANT = 64 * 1024 * 1024 - 64 * 1024
MESH = pl.DeviceIdType.MESH
BF16 = jnp.bfloat16
F32 = jnp.float32


def middle_kernel(
    n, groups,
    starts, lens, volume, depth, colmap, measured, weight,
    out_ref,
    start_ref, len_ref, vol, dcat, maps, meas, rw, meas_t, rw_t, acc, wt, halo, gathered, part, parts_in, own, halo_s, extra,
    vol_sem, dep_sem, loc_sem,
    m_send, m_recv, x_send, x_recv, f_send, f_recv, h_send, h_recv, g_send, g_recv, r_send, r_recv, s_send, s_recv, relay_send, e_send, e_recv,
):
    g = lax.axis_index("gz")
    me = lax.axis_index("gx")
    core = lax.rem(g, 2)
    sibling = g + 1 - 2 * core
    half = lax.rem(g // 2, 2)
    across = g + 2 - 4 * half
    rows = BLK // 2
    cols = maps.shape[2]
    slices = vol.shape[0]
    steps = slices // CHUNK
    t_len = depth.shape[2]

    def my_columns(who):
        return pl.ds(pl.multiple_of(who * cols, 128), cols)

    def x_rows(who):
        return pl.ds(pl.multiple_of(who * BLK, BLK), BLK)

    depth_copies = [
        pltpu.make_async_copy(depth.at[v], dcat.at[:, pl.ds(v * t_len, t_len)], dep_sem.at[v])
        for v in range(VIEWS)
    ]
    for copy in depth_copies:
        copy.start()

    def vol_copy(k):
        return pltpu.make_async_copy(
            volume.at[pl.ds(k * CHUNK, CHUNK)], vol.at[pl.ds(k * CHUNK, CHUNK)], vol_sem.at[k]
        )

    for k in range(steps):
        vol_copy(k).start()
    band_copies = [
        pltpu.make_async_copy(starts, start_ref, loc_sem.at[3]),
        pltpu.make_async_copy(lens, len_ref, loc_sem.at[4]),
    ]
    for copy in band_copies:
        copy.start()
    local_copies = [
        pltpu.make_async_copy(colmap.at[:, :, my_columns(me)], maps.at[:, x_rows(me), :], loc_sem.at[0]),
        pltpu.make_async_copy(measured, meas, loc_sem.at[1]),
        pltpu.make_async_copy(weight, rw, loc_sem.at[2]),
    ]
    for copy in local_copies:
        copy.start()

    barrier = pltpu.get_barrier_semaphore()
    for d in range(1, n):
        pl.semaphore_signal(barrier, inc=1, device_id={"gx": lax.rem(me + d, n)}, device_id_type=MESH)

    @pl.when(g > 0)
    def _():
        pl.semaphore_signal(barrier, inc=1, device_id={"gz": g - 1}, device_id_type=MESH)

    @pl.when(g < groups - 1)
    def _():
        pl.semaphore_signal(barrier, inc=1, device_id={"gz": g + 1}, device_id_type=MESH)

    pl.semaphore_signal(barrier, inc=1, device_id={"gz": across}, device_id_type=MESH)
    below = jnp.where(g > 0, 1, 0)
    above = jnp.where(g < groups - 1, 1, 0)
    pl.semaphore_wait(barrier, n + below + above)

    def piece(view, who, which):
        return maps.at[view, pl.ds(pl.multiple_of(who * BLK + which * rows, rows), rows), :]

    def map_copy(d):
        peer = lax.rem(me + d, n)
        return pltpu.make_async_remote_copy(
            src_ref=colmap.at[core, pl.ds(pl.multiple_of(half * rows, rows), rows), my_columns(peer)],
            dst_ref=piece(core, me, half),
            send_sem=m_send.at[d], recv_sem=m_recv.at[d],
            device_id={"gx": peer}, device_id_type=MESH,
        )

    def across_copy(d, which):
        src = piece(core, lax.rem(me - d + n, n), which)
        return pltpu.make_async_remote_copy(
            src_ref=src, dst_ref=src,
            send_sem=x_send.at[d], recv_sem=x_recv.at[d],
            device_id={"gz": across}, device_id_type=MESH,
        )

    def forward_copy(d, view, came, which):
        src = piece(view, lax.rem(me - d + n, n), which)
        return pltpu.make_async_remote_copy(
            src_ref=src, dst_ref=src,
            send_sem=f_send.at[came, d], recv_sem=f_recv.at[came, d],
            device_id={"gz": sibling}, device_id_type=MESH,
        )

    for d in range(1, n):
        map_copy(d).start()

    def to_below(src, land, send, recv, v):
        return pltpu.make_async_remote_copy(
            src_ref=src, dst_ref=land.at[1, v], send_sem=send.at[0, v], recv_sem=recv.at[0, v],
            device_id={"gz": g - 1}, device_id_type=MESH,
        )

    def to_above(src, land, send, recv, v):
        return pltpu.make_async_remote_copy(
            src_ref=src, dst_ref=land.at[0, v], send_sem=send.at[1, v], recv_sem=recv.at[1, v],
            device_id={"gz": g + 1}, device_id_type=MESH,
        )

    def exchange_start(low_src, high_src, land, send, recv, v):
        @pl.when(g > 0)
        def _():
            to_below(low_src, land, send, recv, v).start()

        @pl.when(g < groups - 1)
        def _():
            to_above(high_src, land, send, recv, v).start()

        @pl.when(g == 0)
        def _():
            land[0, v] = jnp.zeros_like(land[0, v])

        @pl.when(g == groups - 1)
        def _():
            land[1, v] = jnp.zeros_like(land[1, v])

    def exchange_wait(low_src, high_src, land, send, recv, v):
        @pl.when(g > 0)
        def _():
            to_below(low_src, land, send, recv, v).wait_send()
            to_above(high_src, land, send, recv, v).wait_recv()

        @pl.when(g < groups - 1)
        def _():
            to_above(high_src, land, send, recv, v).wait_send()
            to_below(low_src, land, send, recv, v).wait_recv()

    def gather_copy(d, v, slot):
        return pltpu.make_async_remote_copy(
            src_ref=gathered.at[slot, v], dst_ref=gathered.at[slot, v],
            send_sem=g_send.at[v, d], recv_sem=g_recv.at[v, d],
            device_id={"gx": lax.rem(me + d, n)}, device_id_type=MESH,
        )

    def relay_copy(v, end, other):
        return pltpu.make_async_remote_copy(
            src_ref=gathered.at[other, v], dst_ref=gathered.at[other, v],
            send_sem=relay_send.at[v], recv_sem=g_recv.at[v, (end - other) % n],
            device_id={"gx": end}, device_id_type=MESH,
        )

    def each_sent(do, v):
        for d in range(1, n):
            if d == n - 1:
                pl.when(me != 0)(functools.partial(do, d, v))
            elif d == 1:
                pl.when(me != n - 1)(functools.partial(do, d, v))
            else:
                do(d, v)

    acc[...] = jnp.zeros_like(acc)
    for copy in depth_copies + band_copies:
        copy.wait()

    def forward(v, k, carry):
        if v == 0:
            vol_copy(k).wait()
        coarse = vol[pl.ds(k * CHUNK, CHUNK)].astype(BF16).reshape(CHUNK * BLK, vol.shape[2])
        foot = jnp.dot(coarse, dcat[:, v * t_len:(v + 1) * t_len], preferred_element_type=F32)
        sums = [acc[v, b] for b in range(3)]
        for i in range(CHUNK):
            z = k * CHUNK + i
            low = jnp.where(start_ref[v, z] < g * BLK, 1.0, 0.0).astype(F32)
            up = jnp.where(start_ref[v, z] + len_ref[v, z] > (g + 1) * BLK, 1.0, 0.0).astype(F32)
            t = [foot[i * BLK:(i + 1) * BLK, b * BLK:(b + 1) * BLK] for b in range(3)]
            sums[0] = sums[0] + low * t[0]
            sums[1] = sums[1] + low * t[1] + (1.0 - low) * t[0]
            sums[2] = sums[2] + (low * up) * t[2] + ((1.0 - low) * up) * t[1]
        for b in range(3):
            acc[v, b] = sums[b]
        return carry

    for v in range(VIEWS):
        lax.fori_loop(0, steps, functools.partial(forward, v), 0)
        for b in (0, 2):
            wt[b // 2, v] = acc[v, b].T.astype(BF16)
        exchange_start(wt.at[0, v], wt.at[1, v], halo, h_send, h_recv, v)

    def send_window(v):
        window = acc[v, 1].T.astype(BF16).astype(F32)
        exchange_wait(wt.at[0, v], wt.at[1, v], halo, h_send, h_recv, v)
        gathered[me, v] = (window + halo[0, v].astype(F32) + halo[1, v].astype(F32)).astype(BF16)
        each_sent(lambda d, v: gather_copy(d, v, me).start(), v)

    send_window(0)
    for d in range(1, n):
        map_copy(d).wait_recv()
        across_copy(d, half).start()
        forward_copy(d, core, 0, half).start()
    send_window(1)
    for copy in local_copies:
        copy.wait()
    for v in range(VIEWS):
        meas_t[v] = meas[pl.ds(v, cols, stride=VIEWS), :].T
        rw_t[v] = rw[pl.ds(v, cols, stride=VIEWS), :].T
    for d in range(1, n):
        across_copy(d, 1 - half).wait_recv()
        forward_copy(d, core, 1, 1 - half).start()

    def reduce_copy(d, v):
        peer = lax.rem(me + d, n)
        return pltpu.make_async_remote_copy(
            src_ref=part.at[peer, v], dst_ref=parts_in.at[d, v],
            send_sem=r_send.at[v, d], recv_sem=r_recv.at[v, d],
            device_id={"gx": peer}, device_id_type=MESH,
        )

    def extra_copy(v, target, neighbour):
        return pltpu.make_async_remote_copy(
            src_ref=part.at[target, v], dst_ref=extra.at[v],
            send_sem=e_send.at[v], recv_sem=e_recv.at[v],
            device_id={"gx": neighbour}, device_id_type=MESH,
        )

    def start_reduce(d, v):
        if d == n - 2 and d == 2:
            pl.when(jnp.logical_and(me != 1, me != n - 2))(lambda: reduce_copy(d, v).start())
        elif d == n - 2:
            pl.when(me != 1)(lambda: reduce_copy(d, v).start())
        elif d == 2:
            pl.when(me != n - 2)(lambda: reduce_copy(d, v).start())
        else:
            reduce_copy(d, v).start()

    def combine(v):
        for device, target, d in ((1, n - 1, n - 2), (n - 2, 0, 2)):
            @pl.when(me == device)
            def _():
                extra_copy(v, target, 0).wait_recv()
                part[target, v] = (own[target, v] + extra[v].astype(F32)).astype(BF16)
                reduce_copy(d, v).start()

    for v in range(VIEWS):
        first = sorted({2, n - 2})
        for d in first + [d for d in range(1, n) if d not in first]:
            gather_copy(d, v, lax.rem(me - d + n, n)).wait_recv()
            if d == 2:
                pl.when(me == 1)(lambda: relay_copy(v, 0, n - 1).start())
            if d == n - 2:
                pl.when(me == n - 2)(lambda: relay_copy(v, n - 1, 0).start())
        if v == 0:
            for d in range(1, n):
                forward_copy(d, 1 - core, 0, half).wait_recv()
                forward_copy(d, 1 - core, 1, 1 - half).wait_recv()
        else:
            combine(v - 1)
        window = jnp.concatenate([gathered[j, v] for j in range(n)], axis=1)
        projection = jnp.dot(window, maps[v], preferred_element_type=F32)
        residual = (rw_t[v] * (meas_t[v] - projection)).astype(BF16)
        spread = lax.dot_general(residual, maps[v], (((1,), (1,)), ((), ())), preferred_element_type=F32)
        for j in range(n):
            own[j, v] = spread[:, j * BLK:(j + 1) * BLK]
            part[j, v] = spread[:, j * BLK:(j + 1) * BLK].astype(BF16)
        pl.when(me == 0)(lambda: extra_copy(v, n - 1, 1).start())
        pl.when(me == n - 1)(lambda: extra_copy(v, 0, n - 2).start())
        each_sent(start_reduce, v)

    combine(VIEWS - 1)
    for v in range(VIEWS):
        total = own[me, v]
        for d in range(1, n):
            if d in (1, n - 1):
                end = 0 if d == 1 else n - 1

                @pl.when(me != end)
                def _():
                    reduce_copy(d, v).wait_recv()

                @pl.when(me == end)
                def _():
                    parts_in[d, v] = jnp.zeros_like(parts_in[d, v])
            else:
                reduce_copy(d, v).wait_recv()
            total = total + parts_in[d, v].astype(F32)
        halo_s[2, v] = total.T.astype(BF16)
        exchange_start(halo_s.at[2, v], halo_s.at[2, v], halo_s, s_send, s_recv, v)

    out_ref[1] = halo_s[2]
    for v in range(VIEWS):
        exchange_wait(halo_s.at[2, v], halo_s.at[2, v], halo_s, s_send, s_recv, v)
    out_ref[0] = halo_s[0]
    out_ref[2] = halo_s[1]
    for d in range(1, n):
        map_copy(d).wait_send()
        across_copy(d, half).wait_send()
        forward_copy(d, core, 0, half).wait_send()
        forward_copy(d, core, 1, 1 - half).wait_send()
    for v in range(VIEWS):
        each_sent(lambda d, v: gather_copy(d, v, me).wait_send(), v)
        each_sent(lambda d, v: reduce_copy(d, v).wait_send(), v)
        pl.when(me == 1)(lambda: relay_copy(v, 0, n - 1).wait_send())
        pl.when(me == n - 2)(lambda: relay_copy(v, n - 1, 0).wait_send())
        pl.when(me == 0)(lambda: extra_copy(v, n - 1, 1).wait_send())
        pl.when(me == n - 1)(lambda: extra_copy(v, 0, n - 2).wait_send())


def middle(volume, column_map, depth_map, measured, row_weight, band_start, band_len):
    n, groups = lax.axis_size("gx"), lax.axis_size("gz")
    slices, x_columns, y_cells = volume.shape
    views, _, t_len = depth_map.shape
    cols = measured.shape[0]
    hbm = pl.BlockSpec(memory_space=pl.ANY)
    block = (views, BLK, BLK)
    dma = pltpu.SemaphoreType.DMA
    return pl.pallas_call(
        functools.partial(middle_kernel, n, groups),
        out_shape=jax.ShapeDtypeStruct((3, *block), BF16),
        in_specs=[hbm] * 7,
        out_specs=pl.BlockSpec(memory_space=pltpu.VMEM),
        scratch_shapes=[
            pltpu.SMEM((views, slices), jnp.int32),
            pltpu.SMEM((views, slices), jnp.int32),
            pltpu.VMEM((slices, x_columns, y_cells), F32),
            pltpu.VMEM((y_cells, views * t_len), BF16),
            pltpu.VMEM((views, n * BLK, cols), BF16),
            pltpu.VMEM((cols * views, BLK), F32),
            pltpu.VMEM((cols * views, BLK), F32),
            pltpu.VMEM((views, BLK, cols), F32),
            pltpu.VMEM((views, BLK, cols), F32),
            pltpu.VMEM((views, 3, BLK, BLK), F32),
            pltpu.VMEM((2, *block), BF16),
            pltpu.VMEM((2, *block), BF16),
            pltpu.VMEM((n, *block), BF16),
            pltpu.VMEM((n, *block), BF16),
            pltpu.VMEM((n, *block), BF16),
            pltpu.VMEM((n, *block), F32),
            pltpu.VMEM((3, *block), BF16),
            pltpu.VMEM(block, BF16),
            dma((slices // CHUNK,)), dma((views,)), dma((5,)),
            dma((n,)), dma((n,)), dma((n,)), dma((n,)), dma((2, n)), dma((2, n)),
            dma((2, views)), dma((2, views)), dma((views, n)), dma((views, n)),
            dma((views, n)), dma((views, n)), dma((2, views)), dma((2, views)),
            dma((views,)), dma((views,)), dma((views,)),
        ],
        compiler_params=pltpu.CompilerParams(
            collective_id=0, has_side_effects=True, vmem_limit_bytes=GRANT
        ),
        name="project_and_spread",
    )(
        band_start, band_len, volume, depth_map, column_map,
        measured.reshape(cols * views, BLK), row_weight.reshape(cols * views, BLK),
    )


def back_kernel(
    starts, lens, spread_in, depth_in, volume, col_weight, out,
    start_ref, len_ref, spread, depth, vol, cw, images, result,
    in_sem, vol_sem, cw_sem, out_sem,
):
    g = lax.axis_index("gz")
    slices = vol.shape[0]
    first_copies = [
        pltpu.make_async_copy(spread_in, spread, in_sem.at[0]),
        pltpu.make_async_copy(depth_in, depth, in_sem.at[1]),
        pltpu.make_async_copy(starts, start_ref, in_sem.at[2]),
        pltpu.make_async_copy(lens, len_ref, in_sem.at[3]),
    ]
    for copy in first_copies:
        copy.start()

    def part(ref, k):
        return ref.at[pl.ds(k * CHUNK, CHUNK)]

    def vol_copy(k):
        return pltpu.make_async_copy(part(volume, k), part(vol, k), vol_sem.at[k])

    def cw_copy(k):
        return pltpu.make_async_copy(part(col_weight, k), part(cw, k), cw_sem.at[k])

    for k in range(slices // CHUNK):
        vol_copy(k).start()
        cw_copy(k).start()
    for copy in first_copies:
        copy.wait()
    depth_contract = (((1,), (1,)), ((), ()))
    for v in range(VIEWS):
        low = jnp.concatenate([spread[0, v], spread[1, v]], axis=1)
        high = jnp.concatenate([spread[1, v], spread[2, v]], axis=1)
        pair = lax.dot_general(
            jnp.concatenate([low, high], axis=0), depth[v, :, :2 * BLK],
            depth_contract, preferred_element_type=F32,
        )
        images[v, 0] = lax.dot_general(
            spread[1, v], depth[v, :, :BLK], depth_contract, preferred_element_type=F32
        )
        images[v, 1] = pair[:BLK]
        images[v, 2] = pair[BLK:]
        images[v, 3] = pair[:BLK] + lax.dot_general(
            spread[2, v], depth[v, :, 2 * BLK:], depth_contract, preferred_element_type=F32
        )

    def out_copy(z):
        return pltpu.make_async_copy(result.at[z], out.at[z], out_sem.at[z])

    def update(k, carry):
        vol_copy(k).wait()
        cw_copy(k).wait()
        for i in range(CHUNK):
            z = k * CHUNK + i
            total = None
            for v in range(VIEWS):
                low = (start_ref[v, z] < g * BLK).astype(jnp.int32)
                up = (start_ref[v, z] + len_ref[v, z] > (g + 1) * BLK).astype(jnp.int32)
                image = images[v, low + 2 * up]
                total = image if total is None else total + image
            result[z] = vol[z] + cw[z].astype(F32) * total
            out_copy(z).start()
        return carry

    lax.fori_loop(0, slices // CHUNK, update, 0)
    for z in range(slices):
        out_copy(z).wait()


def back(spread, depth_map, volume, col_weight, band_start, band_len):
    slices, x_columns, y_cells = volume.shape
    hbm = pl.BlockSpec(memory_space=pl.ANY)
    dma = pltpu.SemaphoreType.DMA
    return pl.pallas_call(
        back_kernel,
        out_shape=jax.ShapeDtypeStruct(volume.shape, F32),
        in_specs=[hbm] * 6,
        out_specs=hbm,
        scratch_shapes=[
            pltpu.SMEM(band_start.shape, jnp.int32),
            pltpu.SMEM(band_start.shape, jnp.int32),
            pltpu.VMEM(spread.shape, BF16),
            pltpu.VMEM(depth_map.shape, BF16),
            pltpu.VMEM(volume.shape, F32),
            pltpu.VMEM(volume.shape, BF16),
            pltpu.VMEM((VIEWS, 4, x_columns, y_cells), F32),
            pltpu.VMEM(volume.shape, F32),
            dma((4,)), dma((slices // CHUNK,)), dma((slices // CHUNK,)), dma((slices,)),
        ],
        compiler_params=pltpu.CompilerParams(vmem_limit_bytes=GRANT),
        name="backproject",
    )(band_start, band_len, spread, depth_map, volume, col_weight)


def local(volume, col_weight, column_map, depth_map, measured, row_weight, band_start, band_len):
    spread = middle(volume, column_map, depth_map, measured, row_weight, band_start, band_len)
    return back(spread, depth_map, volume, col_weight, band_start, band_len)


def solution(mesh):
    in_specs = (
        P(("grp", "gz"), "gx", None),
        P("gz", "gx", None),
        P(None, "gx", None),
        P(),
        P(("grp", "gx"), None, "gz"),
        P("gx", None, "gz"),
        P(None, "gz"),
        P(None, "gz"),
    )
    out_specs = P(("grp", "gz"), "gx", None)
    return jax.shard_map(local, mesh=mesh, in_specs=in_specs, out_specs=out_specs, check_vma=False)
```

```python
import functools

import jax
import jax.numpy as jnp
from jax import lax
from jax.experimental import pallas as pl
from jax.experimental.pallas import tpu as pltpu
from jax.sharding import PartitionSpec as P

BLK = 128
VIEWS = 2
CHUNK = 4
GRANT = 64 * 1024 * 1024 - 64 * 1024
MESH = pl.DeviceIdType.MESH
BF16 = jnp.bfloat16
F32 = jnp.float32


def middle_kernel(
    n, groups,
    starts, lens, volume, depth, colmap, measured, weight,
    out_ref,
    start_ref, len_ref, vol, dcat, maps, meas, rw, meas_t, rw_t, acc, wt, halo, gathered, part, parts_in, own, halo_s,
    vol_sem, dep_sem, loc_sem,
    m_send, m_recv, x_send, x_recv, f_send, f_recv, h_send, h_recv, g_send, g_recv, r_send, r_recv, s_send, s_recv,
):
    g = lax.axis_index("gz")
    me = lax.axis_index("gx")
    core = lax.rem(g, 2)
    sibling = g + 1 - 2 * core
    half = lax.rem(g // 2, 2)
    across = g + 2 - 4 * half
    rows = BLK // 2
    cols = maps.shape[2]
    slices = vol.shape[0]
    steps = slices // CHUNK
    t_len = depth.shape[2]

    def my_columns(who):
        return pl.ds(pl.multiple_of(who * cols, 128), cols)

    def x_rows(who):
        return pl.ds(pl.multiple_of(who * BLK, BLK), BLK)

    barrier = pltpu.get_barrier_semaphore()
    for d in range(1, n):
        pl.semaphore_signal(barrier, inc=1, device_id={"gx": lax.rem(me + d, n)}, device_id_type=MESH)

    @pl.when(g > 0)
    def _():
        pl.semaphore_signal(barrier, inc=1, device_id={"gz": g - 1}, device_id_type=MESH)

    @pl.when(g < groups - 1)
    def _():
        pl.semaphore_signal(barrier, inc=1, device_id={"gz": g + 1}, device_id_type=MESH)

    pl.semaphore_signal(barrier, inc=1, device_id={"gz": across}, device_id_type=MESH)
    depth_copies = [
        pltpu.make_async_copy(depth.at[v], dcat.at[:, pl.ds(v * t_len, t_len)], dep_sem.at[v])
        for v in range(VIEWS)
    ]
    for copy in depth_copies:
        copy.start()

    def vol_copy(k):
        return pltpu.make_async_copy(
            volume.at[pl.ds(k * CHUNK, CHUNK)], vol.at[pl.ds(k * CHUNK, CHUNK)], vol_sem.at[k]
        )

    for k in range(steps):
        vol_copy(k).start()
    band_copies = [
        pltpu.make_async_copy(starts, start_ref, loc_sem.at[3]),
        pltpu.make_async_copy(lens, len_ref, loc_sem.at[4]),
    ]
    for copy in band_copies:
        copy.start()
    local_copies = [
        pltpu.make_async_copy(colmap.at[:, :, my_columns(me)], maps.at[:, x_rows(me), :], loc_sem.at[0]),
        pltpu.make_async_copy(measured, meas, loc_sem.at[1]),
        pltpu.make_async_copy(weight, rw, loc_sem.at[2]),
    ]
    for copy in local_copies:
        copy.start()

    below = jnp.where(g > 0, 1, 0)
    above = jnp.where(g < groups - 1, 1, 0)
    pl.semaphore_wait(barrier, n + below + above)

    def piece(view, who, which):
        return maps.at[view, pl.ds(pl.multiple_of(who * BLK + which * rows, rows), rows), :]

    def map_copy(d):
        peer = lax.rem(me + d, n)
        return pltpu.make_async_remote_copy(
            src_ref=colmap.at[core, pl.ds(pl.multiple_of(half * rows, rows), rows), my_columns(peer)],
            dst_ref=piece(core, me, half),
            send_sem=m_send.at[d], recv_sem=m_recv.at[d],
            device_id={"gx": peer}, device_id_type=MESH,
        )

    def across_copy(d, which):
        src = piece(core, lax.rem(me - d + n, n), which)
        return pltpu.make_async_remote_copy(
            src_ref=src, dst_ref=src,
            send_sem=x_send.at[d], recv_sem=x_recv.at[d],
            device_id={"gz": across}, device_id_type=MESH,
        )

    def forward_copy(d, view, came, which):
        src = piece(view, lax.rem(me - d + n, n), which)
        return pltpu.make_async_remote_copy(
            src_ref=src, dst_ref=src,
            send_sem=f_send.at[came, d], recv_sem=f_recv.at[came, d],
            device_id={"gz": sibling}, device_id_type=MESH,
        )

    for d in range(1, n):
        map_copy(d).start()

    def to_below(src, land, send, recv, v):
        return pltpu.make_async_remote_copy(
            src_ref=src, dst_ref=land.at[1, v], send_sem=send.at[0, v], recv_sem=recv.at[0, v],
            device_id={"gz": g - 1}, device_id_type=MESH,
        )

    def to_above(src, land, send, recv, v):
        return pltpu.make_async_remote_copy(
            src_ref=src, dst_ref=land.at[0, v], send_sem=send.at[1, v], recv_sem=recv.at[1, v],
            device_id={"gz": g + 1}, device_id_type=MESH,
        )

    def exchange_start(low_src, high_src, land, send, recv, v):
        @pl.when(g > 0)
        def _():
            to_below(low_src, land, send, recv, v).start()

        @pl.when(g < groups - 1)
        def _():
            to_above(high_src, land, send, recv, v).start()

        @pl.when(g == 0)
        def _():
            land[0, v] = jnp.zeros_like(land[0, v])

        @pl.when(g == groups - 1)
        def _():
            land[1, v] = jnp.zeros_like(land[1, v])

    def exchange_wait(low_src, high_src, land, send, recv, v):
        @pl.when(g > 0)
        def _():
            to_below(low_src, land, send, recv, v).wait_send()
            to_above(high_src, land, send, recv, v).wait_recv()

        @pl.when(g < groups - 1)
        def _():
            to_above(high_src, land, send, recv, v).wait_send()
            to_below(low_src, land, send, recv, v).wait_recv()

    def gather_copy(d, v, slot):
        return pltpu.make_async_remote_copy(
            src_ref=gathered.at[slot, v], dst_ref=gathered.at[slot, v],
            send_sem=g_send.at[v, d], recv_sem=g_recv.at[v, d],
            device_id={"gx": lax.rem(me + d, n)}, device_id_type=MESH,
        )

    def each_sent(do, v):
        for d in range(1, n):
            do(d, v)

    acc[...] = jnp.zeros_like(acc)
    for copy in depth_copies + band_copies:
        copy.wait()

    def forward(v, k, carry):
        if v == 0:
            vol_copy(k).wait()
        coarse = vol[pl.ds(k * CHUNK, CHUNK)].astype(BF16).reshape(CHUNK * BLK, vol.shape[2])
        foot = jnp.dot(coarse, dcat[:, v * t_len:(v + 1) * t_len], preferred_element_type=F32)
        sums = [acc[v, b] for b in range(3)]
        for i in range(CHUNK):
            z = k * CHUNK + i
            low = jnp.where(start_ref[v, z] < g * BLK, 1.0, 0.0).astype(F32)
            up = jnp.where(start_ref[v, z] + len_ref[v, z] > (g + 1) * BLK, 1.0, 0.0).astype(F32)
            t = [foot[i * BLK:(i + 1) * BLK, b * BLK:(b + 1) * BLK] for b in range(3)]
            sums[0] = sums[0] + low * t[0]
            sums[1] = sums[1] + low * t[1] + (1.0 - low) * t[0]
            sums[2] = sums[2] + (low * up) * t[2] + ((1.0 - low) * up) * t[1]
        for b in range(3):
            acc[v, b] = sums[b]
        return carry

    for v in range(VIEWS):
        lax.fori_loop(0, steps, functools.partial(forward, v), 0)
        for b in (0, 2):
            wt[b // 2, v] = acc[v, b].T.astype(BF16)
        exchange_start(wt.at[0, v], wt.at[1, v], halo, h_send, h_recv, v)

    def send_window(v):
        window = acc[v, 1].T.astype(BF16).astype(F32)
        exchange_wait(wt.at[0, v], wt.at[1, v], halo, h_send, h_recv, v)
        gathered[me, v] = (window + halo[0, v].astype(F32) + halo[1, v].astype(F32)).astype(BF16)
        each_sent(lambda d, v: gather_copy(d, v, me).start(), v)

    for d in range(1, n):
        map_copy(d).wait_recv()
        across_copy(d, half).start()
        forward_copy(d, core, 0, half).start()
    send_window(0)
    send_window(1)
    for copy in local_copies:
        copy.wait()
    for v in range(VIEWS):
        meas_t[v] = meas[pl.ds(v, cols, stride=VIEWS), :].T
        rw_t[v] = rw[pl.ds(v, cols, stride=VIEWS), :].T
    for d in range(1, n):
        across_copy(d, 1 - half).wait_recv()
        forward_copy(d, core, 1, 1 - half).start()

    def reduce_copy(d, v):
        peer = lax.rem(me + d, n)
        return pltpu.make_async_remote_copy(
            src_ref=part.at[peer, v], dst_ref=parts_in.at[d, v],
            send_sem=r_send.at[v, d], recv_sem=r_recv.at[v, d],
            device_id={"gx": peer}, device_id_type=MESH,
        )

    for v in range(VIEWS):
        for d in range(1, n):
            gather_copy(d, v, lax.rem(me - d + n, n)).wait_recv()
        if v == 0:
            for d in range(1, n):
                forward_copy(d, 1 - core, 0, half).wait_recv()
                forward_copy(d, 1 - core, 1, 1 - half).wait_recv()
        window = jnp.concatenate([gathered[j, v] for j in range(n)], axis=1)
        projection = jnp.dot(window, maps[v], preferred_element_type=F32)
        residual = (rw_t[v] * (meas_t[v] - projection)).astype(BF16)
        spread = lax.dot_general(residual, maps[v], (((1,), (1,)), ((), ())), preferred_element_type=F32)
        for j in range(n):
            own[j, v] = spread[:, j * BLK:(j + 1) * BLK]
            part[j, v] = spread[:, j * BLK:(j + 1) * BLK].astype(BF16)
        each_sent(lambda d, v: reduce_copy(d, v).start(), v)

    for v in range(VIEWS):
        total = own[me, v]
        for d in range(1, n):
            reduce_copy(d, v).wait_recv()
            total = total + parts_in[d, v].astype(F32)
        halo_s[2, v] = total.T.astype(BF16)
        exchange_start(halo_s.at[2, v], halo_s.at[2, v], halo_s, s_send, s_recv, v)

    out_ref[1] = halo_s[2]
    for v in range(VIEWS):
        exchange_wait(halo_s.at[2, v], halo_s.at[2, v], halo_s, s_send, s_recv, v)
    out_ref[0] = halo_s[0]
    out_ref[2] = halo_s[1]
    for d in range(1, n):
        map_copy(d).wait_send()
        across_copy(d, half).wait_send()
        forward_copy(d, core, 0, half).wait_send()
        forward_copy(d, core, 1, 1 - half).wait_send()
    for v in range(VIEWS):
        each_sent(lambda d, v: gather_copy(d, v, me).wait_send(), v)
        each_sent(lambda d, v: reduce_copy(d, v).wait_send(), v)


def middle(volume, column_map, depth_map, measured, row_weight, band_start, band_len):
    n, groups = lax.axis_size("gx"), lax.axis_size("gz")
    slices, x_columns, y_cells = volume.shape
    views, _, t_len = depth_map.shape
    cols = measured.shape[0]
    hbm = pl.BlockSpec(memory_space=pl.ANY)
    block = (views, BLK, BLK)
    dma = pltpu.SemaphoreType.DMA
    return pl.pallas_call(
        functools.partial(middle_kernel, n, groups),
        out_shape=jax.ShapeDtypeStruct((3, *block), BF16),
        in_specs=[hbm] * 7,
        out_specs=pl.BlockSpec(memory_space=pltpu.VMEM),
        scratch_shapes=[
            pltpu.SMEM((views, slices), jnp.int32),
            pltpu.SMEM((views, slices), jnp.int32),
            pltpu.VMEM((slices, x_columns, y_cells), F32),
            pltpu.VMEM((y_cells, views * t_len), BF16),
            pltpu.VMEM((views, n * BLK, cols), BF16),
            pltpu.VMEM((cols * views, BLK), F32),
            pltpu.VMEM((cols * views, BLK), F32),
            pltpu.VMEM((views, BLK, cols), F32),
            pltpu.VMEM((views, BLK, cols), F32),
            pltpu.VMEM((views, 3, BLK, BLK), F32),
            pltpu.VMEM((2, *block), BF16),
            pltpu.VMEM((2, *block), BF16),
            pltpu.VMEM((n, *block), BF16),
            pltpu.VMEM((n, *block), BF16),
            pltpu.VMEM((n, *block), BF16),
            pltpu.VMEM((n, *block), F32),
            pltpu.VMEM((3, *block), BF16),
            dma((slices // CHUNK,)), dma((views,)), dma((5,)),
            dma((n,)), dma((n,)), dma((n,)), dma((n,)), dma((2, n)), dma((2, n)),
            dma((2, views)), dma((2, views)), dma((views, n)), dma((views, n)),
            dma((views, n)), dma((views, n)), dma((2, views)), dma((2, views)),
        ],
        compiler_params=pltpu.CompilerParams(
            collective_id=0, has_side_effects=True, vmem_limit_bytes=GRANT
        ),
        name="project_and_spread",
    )(
        band_start, band_len, volume, depth_map, column_map,
        measured.reshape(cols * views, BLK), row_weight.reshape(cols * views, BLK),
    )


def back_kernel(
    starts, lens, spread_in, depth_in, volume, col_weight, out,
    start_ref, len_ref, spread, depth, vol, cw, images, result,
    in_sem, vol_sem, cw_sem, out_sem,
):
    g = lax.axis_index("gz")
    slices = vol.shape[0]
    first_copies = [
        pltpu.make_async_copy(spread_in, spread, in_sem.at[0]),
        pltpu.make_async_copy(depth_in, depth, in_sem.at[1]),
        pltpu.make_async_copy(starts, start_ref, in_sem.at[2]),
        pltpu.make_async_copy(lens, len_ref, in_sem.at[3]),
    ]
    for copy in first_copies:
        copy.start()

    def part(ref, k):
        return ref.at[pl.ds(k * CHUNK, CHUNK)]

    def vol_copy(k):
        return pltpu.make_async_copy(part(volume, k), part(vol, k), vol_sem.at[k])

    def cw_copy(k):
        return pltpu.make_async_copy(part(col_weight, k), part(cw, k), cw_sem.at[k])

    for k in range(slices // CHUNK):
        vol_copy(k).start()
        cw_copy(k).start()
    for copy in first_copies:
        copy.wait()
    depth_contract = (((1,), (1,)), ((), ()))
    for v in range(VIEWS):
        low = jnp.concatenate([spread[0, v], spread[1, v]], axis=1)
        high = jnp.concatenate([spread[1, v], spread[2, v]], axis=1)
        pair = lax.dot_general(
            jnp.concatenate([low, high], axis=0), depth[v, :, :2 * BLK],
            depth_contract, preferred_element_type=F32,
        )
        images[v, 0] = lax.dot_general(
            spread[1, v], depth[v, :, :BLK], depth_contract, preferred_element_type=F32
        )
        images[v, 1] = pair[:BLK]
        images[v, 2] = pair[BLK:]
        images[v, 3] = pair[:BLK] + lax.dot_general(
            spread[2, v], depth[v, :, 2 * BLK:], depth_contract, preferred_element_type=F32
        )

    def out_copy(z):
        return pltpu.make_async_copy(result.at[z], out.at[z], out_sem.at[z])

    def update(k, carry):
        vol_copy(k).wait()
        cw_copy(k).wait()
        for i in range(CHUNK):
            z = k * CHUNK + i
            total = None
            for v in range(VIEWS):
                low = (start_ref[v, z] < g * BLK).astype(jnp.int32)
                up = (start_ref[v, z] + len_ref[v, z] > (g + 1) * BLK).astype(jnp.int32)
                image = images[v, low + 2 * up]
                total = image if total is None else total + image
            result[z] = vol[z] + cw[z].astype(F32) * total
            out_copy(z).start()
        return carry

    lax.fori_loop(0, slices // CHUNK, update, 0)
    for z in range(slices):
        out_copy(z).wait()


def back(spread, depth_map, volume, col_weight, band_start, band_len):
    slices, x_columns, y_cells = volume.shape
    hbm = pl.BlockSpec(memory_space=pl.ANY)
    dma = pltpu.SemaphoreType.DMA
    return pl.pallas_call(
        back_kernel,
        out_shape=jax.ShapeDtypeStruct(volume.shape, F32),
        in_specs=[hbm] * 6,
        out_specs=hbm,
        scratch_shapes=[
            pltpu.SMEM(band_start.shape, jnp.int32),
            pltpu.SMEM(band_start.shape, jnp.int32),
            pltpu.VMEM(spread.shape, BF16),
            pltpu.VMEM(depth_map.shape, BF16),
            pltpu.VMEM(volume.shape, F32),
            pltpu.VMEM(volume.shape, BF16),
            pltpu.VMEM((VIEWS, 4, x_columns, y_cells), F32),
            pltpu.VMEM(volume.shape, F32),
            dma((4,)), dma((slices // CHUNK,)), dma((slices // CHUNK,)), dma((slices,)),
        ],
        compiler_params=pltpu.CompilerParams(vmem_limit_bytes=GRANT),
        name="backproject",
    )(band_start, band_len, spread, depth_map, volume, col_weight)


def local(volume, col_weight, column_map, depth_map, measured, row_weight, band_start, band_len):
    spread = middle(volume, column_map, depth_map, measured, row_weight, band_start, band_len)
    return back(spread, depth_map, volume, col_weight, band_start, band_len)


def solution(mesh):
    in_specs = (
        P(("grp", "gz"), "gx", None),
        P("gz", "gx", None),
        P(None, "gx", None),
        P(),
        P(("grp", "gx"), None, "gz"),
        P("gx", None, "gz"),
        P(None, "gz"),
        P(None, "gz"),
    )
    out_specs = P(("grp", "gz"), "gx", None)
    return jax.shard_map(local, mesh=mesh, in_specs=in_specs, out_specs=out_specs, check_vma=False)
```
